32 devices in a mesh: groups: 2 (over y), seq: 16 (over z, x, core).
Axes of the slice: x: 2, y: 2, z: 4, core: 2. Of those that a mesh axis runs over, the one named last changes fastest.
Arguments:
- queries: bfloat16 [4096, 24, 128], P(('groups', 'seq')), parts along dimension 0, may hold values from -72 to 72
- key_heads: bfloat16 [4096, 4, 128], P(('groups', 'seq')), parts along dimension 0, may hold values from -4 to 4
- value_heads: bfloat16 [4096, 4, 128], P(('groups', 'seq')), parts along dimension 0, may hold values from -6 to 6
- grad_out: bfloat16 [4096, 24, 128], P(('groups', 'seq')), parts along dimension 0, may hold values from -6 to 6
- offsets: int32 [2], replicated, may hold values from 1 to 8, as said below
- random_masks: int32 [1], replicated, may hold values from 1 to 15
- global_blocks: int32 [1], replicated, may hold values from 0 to 15
Outputs:
- attended: bfloat16 [4096, 24, 128], P(('groups', 'seq')), parts along dimension 0
- grad_queries: bfloat16 [4096, 24, 128], P(('groups', 'seq')), parts along dimension 0
- grad_keys: bfloat16 [4096, 4, 128], P(('groups', 'seq')), parts along dimension 0
- grad_values: bfloat16 [4096, 4, 128], P(('groups', 'seq')), parts along dimension 0
The draws below stay inside these ranges and needn't reach their ends.
There are 2 independent parts, one for each index of `groups`. The reference program is written for one: setup_inputs(seed, part) draws one part's arguments, and reference() takes and returns one part's arrays. A program takes and returns all parts, laid end to end along the dimension named above; an argument that names none is the same for every part. Nothing has to cross between parts.
Inputs may be any that keep to these rules, and one draw needn't show every extreme that they name: `offsets`: distinct powers of two; one of them is 8.
All inputs are finite; a program needn't handle non-finite values.
Results may differ from the reference program's by a relative error of at most 0.012.
Values may be sent and summed in bfloat16 or wider, within the bound.
A program may use at most 64 MiB of HBM per device.

```python
import jax
import jax.numpy as jnp
from jax import lax

HEADS = 24
KVH = 4
HD = 128
BLK = 128
LEVELS = 2
RAND = 1
GLOB = 1
NBLK = 16
TOKENS = 2048
GROUPED = 6


def shared_keys(key):
    base = jnp.clip(jax.random.normal(jax.random.fold_in(key, 11), (NBLK, BLK, KVH, HD), jnp.float32), -4.0, 4.0)
    return base


def draw_key_heads(key, part):
    return shared_keys(key).reshape(TOKENS, KVH, HD).astype(jnp.bfloat16)


def draw_queries(key, part):
    noise = jnp.clip(jax.random.normal(jax.random.fold_in(key, 23), (NBLK, BLK, HEADS, HD), jnp.float32), -4.0, 4.0)
    return noise.reshape(TOKENS, HEADS, HD).astype(jnp.bfloat16)


def draw_offsets(key, part):
    width_bits = NBLK.bit_length() - 1
    lower = jax.random.permutation(jax.random.fold_in(key, 31), width_bits - 1)[:LEVELS - 1].astype(jnp.int32)
    chosen = jnp.concatenate([lower, jnp.full((1,), width_bits - 1, jnp.int32)])
    chosen = jax.random.permutation(jax.random.fold_in(key, 37), chosen).astype(jnp.int32)
    return jnp.left_shift(jnp.ones((LEVELS,), jnp.int32), chosen)


def shard_levels(own_key, shape, pieces, smallest, high):
    loudness, own = 1.0, jax.random.fold_in(own_key, 6)
    for dim, blocks in pieces:
        heights = jnp.exp(jax.random.uniform(jax.random.fold_in(own, dim), (blocks,), jnp.float32, smallest / len(pieces), high / len(pieces)))
        loudness = loudness * jnp.repeat(heights, shape[dim] // blocks).reshape([-1 if axis == dim else 1 for axis in range(len(shape))])
    return loudness


def centred(stream_key, dims, deviation, most, shards=(), held_as=jnp.bfloat16):
    values = deviation * jax.random.normal(stream_key, dims, jnp.float32)
    if shards:
        values = values * shard_levels(stream_key, dims, shards, -0.22, 0.18)
    return jnp.clip(values, -most, most).astype(held_as)


def setup_inputs(seed: int = 0, part: int = 0) -> dict:
    seeds = jax.random.split(jax.random.key(seed), 8)
    own_keys = jax.random.split(jax.random.fold_in(seeds[7], part), 8)
    return {
        "queries": draw_queries(jax.random.fold_in(jax.random.fold_in(seeds[7], part), 71), part),
        "key_heads": draw_key_heads(jax.random.fold_in(jax.random.fold_in(seeds[7], part), 71), part),
        "value_heads": centred(own_keys[2], (TOKENS, KVH, HD), 1.0, 6.0, ((0, 16),)),
        "grad_out": centred(own_keys[3], (TOKENS, HEADS, HD), 1.0, 6.0, ((0, 16),)),
        "offsets": draw_offsets(jax.random.fold_in(seeds[7], 71), part),
        "random_masks": jax.random.randint(seeds[5], (RAND,), 1, NBLK).astype(jnp.int32),
        "global_blocks": jax.random.randint(seeds[6], (GLOB,), 0, NBLK).astype(jnp.int32),
    }


def forward_head(query_part, key_part, value_part):
    scale = query_part.shape[-1] ** -0.5
    scores = jnp.einsum('qpd,kd->pqk', query_part.astype(jnp.float32), key_part.astype(jnp.float32)) * scale
    top_score = jnp.max(scores, axis=-1, keepdims=True)
    log_total = top_score[..., 0] + jnp.log(jnp.sum(jnp.exp(scores - top_score), axis=-1))
    probs = jnp.exp(scores - log_total[..., None]).astype(jnp.bfloat16)
    output_part = jnp.einsum('pqk,kd->qpd', probs.astype(jnp.float32), value_part.astype(jnp.float32))
    return output_part.astype(jnp.bfloat16), log_total


def backward_head(query_part, key_part, value_part, grad_part, output_part, log_total):
    scale = query_part.shape[-1] ** -0.5
    scores = jnp.einsum('qpd,kd->pqk', query_part.astype(jnp.float32), key_part.astype(jnp.float32)) * scale
    weights = jnp.exp(scores - log_total[..., None])
    probs = weights.astype(jnp.bfloat16)
    deltas = jnp.sum(grad_part.astype(jnp.float32) * output_part.astype(jnp.float32), axis=-1).T
    value_terms = jnp.einsum('pqk,qpd->kd', probs.astype(jnp.float32), grad_part.astype(jnp.float32))
    grad_probs = jnp.einsum('qpd,kd->pqk', grad_part.astype(jnp.float32), value_part.astype(jnp.float32))
    grad_scores = (weights * (grad_probs - deltas[..., None])).astype(jnp.bfloat16)
    grad_query = jnp.einsum('pqk,kd->qpd', grad_scores.astype(jnp.float32), key_part.astype(jnp.float32)) * scale
    key_terms = jnp.einsum('pqk,qpd->kd', grad_scores.astype(jnp.float32), query_part.astype(jnp.float32)) * scale
    return grad_query.astype(jnp.bfloat16), key_terms, value_terms


def reference(queries, key_heads, value_heads, grad_out, offsets, random_masks, global_blocks):
    query_blocks = queries.reshape(NBLK, BLK, KVH, GROUPED, HD)
    grad_blocks = grad_out.reshape(NBLK, BLK, KVH, GROUPED, HD)
    key_blocks = key_heads.reshape(NBLK, BLK, KVH, HD)
    value_blocks = value_heads.reshape(NBLK, BLK, KVH, HD)
    listed = 1 + LEVELS + RAND + GLOB

    def visit(totals, block):
        block = block.astype(jnp.int32)
        chosen = jnp.concatenate([block[None], jnp.bitwise_xor(block, offsets), jnp.bitwise_xor(block, random_masks), global_blocks]).astype(jnp.int32)
        keys_all = key_blocks[chosen].reshape(listed * BLK, KVH, HD).transpose(1, 0, 2)
        values_all = value_blocks[chosen].reshape(listed * BLK, KVH, HD).transpose(1, 0, 2)
        query_part = query_blocks[block].transpose(1, 0, 2, 3)
        grad_part = grad_blocks[block].transpose(1, 0, 2, 3)
        output_part, log_total = jax.vmap(forward_head)(query_part, keys_all, values_all)
        grad_query, key_terms, value_terms = jax.vmap(backward_head)(query_part, keys_all, values_all, grad_part, output_part, log_total)
        terms = jnp.stack([key_terms, value_terms]).reshape(2, KVH, listed, BLK, HD).transpose(2, 0, 3, 1, 4)
        totals = totals.at[chosen].add(terms)
        return totals, (output_part.transpose(1, 0, 2, 3), grad_query.transpose(1, 0, 2, 3))

    start = jnp.zeros((NBLK, 2, BLK, KVH, HD), jnp.float32)
    totals, (outputs, grads) = lax.scan(visit, start, jnp.arange(NBLK, dtype=jnp.int32))
    attended = outputs.reshape(TOKENS, HEADS, HD)
    grad_queries = grads.reshape(TOKENS, HEADS, HD)
    grad_keys = totals[:, 0].reshape(TOKENS, KVH, HD).astype(jnp.bfloat16)
    grad_values = totals[:, 1].reshape(TOKENS, KVH, HD).astype(jnp.bfloat16)
    return (attended, grad_queries, grad_keys, grad_values)
```

```python
import jax
import jax.numpy as jnp
from jax import lax
from jax.experimental import pallas as pl
from jax.experimental.pallas import tpu as pltpu
from jax.sharding import PartitionSpec as P


def from_partner(x, axis, distance):
    return lax.ppermute(x, axis, [(i, i ^ 1 << distance) for i in range(lax.axis_size(axis))])


def broadcast(value, axis, source):
    kept = jnp.where(lax.axis_index(axis) == source, value, 0).astype(value.dtype)
    return lax.psum(kept, axis)


def forward_head(inputs):
    query_part, key_part, value_part = inputs
    scale = query_part.shape[-1] ** (-0.5)
    scores = (
        jnp.einsum("qpd,kd->pqk", query_part, key_part, preferred_element_type=jnp.float32) * scale
    )
    top_score = jnp.max(scores, axis=-1, keepdims=True)
    log_total = top_score[..., 0] + jnp.log(jnp.sum(jnp.exp(scores - top_score), axis=-1))
    probs = jnp.exp(scores - log_total[..., None]).astype(jnp.bfloat16)
    output_part = jnp.einsum("pqk,kd->qpd", probs, value_part, preferred_element_type=jnp.float32)
    return (output_part.astype(jnp.bfloat16), log_total)


def backward_head(inputs):
    query_part, key_part, value_part, grad_part, output_part, log_total = inputs
    scale = query_part.shape[-1] ** (-0.5)
    scores = (
        jnp.einsum("qpd,kd->pqk", query_part, key_part, preferred_element_type=jnp.float32) * scale
    )
    weights = jnp.exp(scores - log_total[..., None])
    probs = weights.astype(jnp.bfloat16)
    deltas = jnp.sum(grad_part.astype(jnp.float32) * output_part.astype(jnp.float32), axis=-1).T
    value_terms = jnp.einsum("pqk,qpd->kd", probs, grad_part, preferred_element_type=jnp.float32)
    grad_probs = jnp.einsum(
        "qpd,kd->pqk", grad_part, value_part, preferred_element_type=jnp.float32
    )
    grad_scores = (weights * (grad_probs - deltas[..., None])).astype(jnp.bfloat16)
    grad_query = (
        jnp.einsum("pqk,kd->qpd", grad_scores, key_part, preferred_element_type=jnp.float32) * scale
    )
    key_terms = (
        jnp.einsum("pqk,qpd->kd", grad_scores, query_part, preferred_element_type=jnp.float32)
        * scale
    )
    return (grad_query.astype(jnp.bfloat16), key_terms, value_terms)


def kv_hop(tensor, bit_number):
    return from_partner(tensor, "seq", bit_number)


def grad_hop(tensor, bit_number):
    return from_partner(tensor.astype(jnp.bfloat16), "seq", bit_number).astype(tensor.dtype)


def bit_sequence():
    width_bits = lax.axis_size("seq").bit_length() - 1
    return list(range(width_bits))


def route(tensor, distance, hop):
    for bit_number in bit_sequence():
        tensor = lax.cond(
            jnp.bitwise_and(jnp.right_shift(distance, bit_number), 1) == 1,
            lambda moved, bit_number=bit_number: hop(moved, bit_number),
            lambda moved: moved,
            tensor,
        )
    return tensor


def fetch_blocks(stacked, distances, global_blocks):
    fetched = [stacked]
    for position in range(distances.shape[0]):
        fetched.append(route(stacked, distances[position], kv_hop))
    position = 0
    fetched.append(broadcast(stacked, "seq", global_blocks[position]))
    return jnp.stack(fetched)


def head_major(fetched, which):
    listed, rows, kv_count, width = (
        fetched.shape[0],
        fetched.shape[2],
        fetched.shape[3],
        fetched.shape[4],
    )
    return fetched[:, which].reshape(listed * rows, kv_count, width).transpose(1, 0, 2)


def local_any(queries, key_heads, value_heads, grad_out, offsets, random_masks, global_blocks):
    rows, heads, width = queries.shape
    kv_count = key_heads.shape[1]
    grouped = heads // kv_count
    distances = jnp.concatenate([offsets, random_masks])
    routed_count = distances.shape[0]
    stacked = jnp.stack([key_heads, value_heads])
    query_part = queries.reshape(rows, kv_count, grouped, width).transpose(1, 0, 2, 3)
    grad_part = grad_out.reshape(rows, kv_count, grouped, width).transpose(1, 0, 2, 3)
    fetched = fetch_blocks(stacked, distances, global_blocks)
    output_part, log_total = lax.map(
        forward_head, (query_part, head_major(fetched, 0), head_major(fetched, 1))
    )
    listed = fetched.shape[0]
    grad_query, key_terms, value_terms = lax.map(
        backward_head,
        (
            query_part,
            head_major(fetched, 0),
            head_major(fetched, 1),
            grad_part,
            output_part,
            log_total,
        ),
    )
    terms = (
        jnp.stack([key_terms, value_terms])
        .reshape(2, kv_count, listed, rows, width)
        .transpose(2, 0, 3, 1, 4)
    )
    totals = terms[0]
    for position in range(routed_count):
        totals = totals + route(terms[1 + position], distances[position], grad_hop)
    summed = lax.psum(terms[1 + routed_count :], "seq")
    owner = lax.axis_index("seq")
    position = 0
    totals = totals + jnp.where(
        owner == global_blocks[position], summed[position], jnp.float32(0.0)
    )
    attended = output_part.transpose(1, 0, 2, 3).reshape(rows, heads, width)
    grad_queries = grad_query.transpose(1, 0, 2, 3).reshape(rows, heads, width)
    grad_keys = totals[0].astype(jnp.bfloat16)
    grad_values = totals[1].astype(jnp.bfloat16)
    return (attended, grad_queries, grad_keys, grad_values)


MESH = pl.DeviceIdType.MESH
FLOAT = jnp.float32
HALF = jnp.bfloat16
FAR, SIDE, CORES = 4, 2, 2


def place():
    me = lax.axis_index("seq")
    return me, me // 4, (me // 2) % 2, me % 2


def neighbours(me, z, x, c):
    sibling = me + 1 - 2 * c
    across = me + 2 - 4 * x
    return sibling, across, me + 4, me - 4


def greet(me, z, x, c):
    sibling, across, up, down = neighbours(me, z, x, c)
    barrier = pltpu.get_barrier_semaphore()
    for other in (sibling, across):
        pl.semaphore_signal(barrier, inc=1, device_id={"seq": other}, device_id_type=MESH)

    @pl.when(z < FAR - 1)
    def _():
        pl.semaphore_signal(barrier, inc=1, device_id={"seq": up}, device_id_type=MESH)

    @pl.when(z > 0)
    def _():
        pl.semaphore_signal(barrier, inc=1, device_id={"seq": down}, device_id_type=MESH)

    pl.semaphore_wait(barrier, 3 + (z + 1) // 2 % 2)


def gather_kernel(kv_ref, all_ref, own_sem, side_sem, core_sem, up_sem, down_sem, recv_sem):
    me, z, x, c = place()
    sibling, across, up, down = neighbours(me, z, x, c)

    def copy(slot, half, sem, target, own=False):
        return pltpu.make_async_remote_copy(
            src_ref=kv_ref.at[half] if own else all_ref.at[slot, half],
            dst_ref=all_ref.at[slot, half],
            send_sem=sem,
            recv_sem=recv_sem.at[slot, half],
            device_id={"seq": target},
            device_id_type=MESH,
        )

    def arrived(slot, half):
        copy(slot, half, side_sem.at[0, half], across).wait_recv()

    def column(row):
        return row * 4 + x * 2 + c

    def opposite(row):
        return row * 4 + (1 - x) * 2 + c

    greet(me, z, x, c)

    def pass_on(row, half, upward, downward, own=False):
        slot = column(row)
        copy(slot, half, side_sem.at[row, half], across, own).start()
        if upward:

            @pl.when(z < FAR - 1)
            def _():
                copy(slot, half, up_sem.at[row, half], up, own).start()

        if downward:

            @pl.when(z > 0)
            def _():
                copy(slot, half, down_sem.at[row, half], down, own).start()

        copy(slot, half, core_sem.at[0, row, half], sibling, own).start()

    for half in range(2):
        pass_on(z, half, True, True, own=True)
        pltpu.make_async_copy(kv_ref.at[half], all_ref.at[me, half], own_sem.at[half]).start()

    def share(row, half):
        arrived(opposite(row), half)
        copy(opposite(row), half, core_sem.at[1, row, half], sibling).start()

    for step in range(1, FAR):
        for half in range(2):

            @pl.when(z - step >= 0)
            def _(step=step, half=half):
                arrived(column(z - step), half)
                pass_on(z - step, half, True, False)

            @pl.when(z + step < FAR)
            def _(step=step, half=half):
                arrived(column(z + step), half)
                pass_on(z + step, half, False, True)

            if step == 1:
                share(z, half)
            else:

                @pl.when(z - step + 1 >= 0)
                def _(step=step, half=half):
                    share(z - step + 1, half)

                @pl.when(z + step - 1 < FAR)
                def _(step=step, half=half):
                    share(z + step - 1, half)

    for half in range(2):

        @pl.when(z - FAR + 1 >= 0)
        def _(half=half):
            share(z - FAR + 1, half)

        @pl.when(z + FAR - 1 < FAR)
        def _(half=half):
            share(z + FAR - 1, half)

    for half in range(2):
        for row in range(FAR):
            for col in range(SIDE):
                arrived(row * 4 + col * 2 + 1 - c, half)
    for half in range(2):
        pltpu.make_async_copy(kv_ref.at[half], all_ref.at[me, half], own_sem.at[half]).wait()
        for row in range(FAR):
            copy(column(row), half, side_sem.at[row, half], across).wait_send()
            for which in range(2):
                copy(column(row), half, core_sem.at[which, row, half], sibling).wait_send()

            @pl.when((z < FAR - 1) & (z >= row))
            def _(row=row, half=half):
                copy(column(row), half, up_sem.at[row, half], up).wait_send()

            @pl.when((z > 0) & (z <= row))
            def _(row=row, half=half):
                copy(column(row), half, down_sem.at[row, half], down).wait_send()


def gather(kv):
    dma = pltpu.SemaphoreType.DMA
    return pl.pallas_call(
        gather_kernel,
        out_shape=jax.ShapeDtypeStruct((16, *kv.shape), kv.dtype),
        in_specs=[pl.BlockSpec(memory_space=pl.ANY)],
        out_specs=pl.BlockSpec(memory_space=pl.ANY),
        scratch_shapes=[
            dma((2,)),
            dma((FAR, 2)),
            dma((2, FAR, 2)),
            dma((FAR, 2)),
            dma((FAR, 2)),
            dma((16, 2)),
        ],
        compiler_params=pltpu.CompilerParams(collective_id=0, has_side_effects=True),
    )(kv)


def nt(a, b):
    return lax.dot_general(a, b, (((1,), (1,)), ((), ())), preferred_element_type=FLOAT)


def nn(a, b):
    return lax.dot_general(a, b, (((1,), (0,)), ((), ())), preferred_element_type=FLOAT)


def attend_kernel(
    chosen_ref, q_ref, g_ref, all_ref,
    att_ref, dq_ref, own_ref, terms_ref,
    qf, gf, af, df, sums,
):
    listed = chosen_ref.shape[0]
    kv_count, rows, width = all_ref.shape[2], all_ref.shape[3], all_ref.shape[4]
    heads = q_ref.shape[0] // rows
    grouped = heads // kv_count
    scale = width ** (-0.5)
    qf[...] = q_ref[...].astype(FLOAT)
    gf[...] = g_ref[...].astype(FLOAT)
    terms_ref[...] = jnp.zeros_like(terms_ref)

    def group(kv, _):
        keys = jnp.concatenate([all_ref[chosen_ref[i], 0, kv] for i in range(listed)], axis=0)
        values = jnp.concatenate([all_ref[chosen_ref[i], 1, kv] for i in range(listed)], axis=0)
        keys_t, values_t = keys.T, values.T
        for pair in range(grouped // 2):
            first = kv * grouped + 2 * pair
            spans = [pl.ds(first + i, rows, stride=heads) for i in range(2)]
            query = jnp.concatenate([qf[s, :] for s in spans], axis=0).astype(HALF)
            grad = jnp.concatenate([gf[s, :] for s in spans], axis=0).astype(HALF)
            scores = nt(keys, query)
            top = jnp.max(scores, axis=0, keepdims=True)
            weights = jnp.exp((scores - top) * scale)
            weights = weights * (1.0 / jnp.sum(weights, axis=0, keepdims=True))
            probs = weights.astype(HALF)
            out = nn(values_t, probs).T
            grad_probs = nt(values, grad)
            deltas = jnp.sum(weights * grad_probs, axis=0, keepdims=True)
            grad_scores = (weights * (grad_probs - deltas)).astype(HALF)
            grad_query = (nn(keys_t, grad_scores) * scale).T
            for i, s in enumerate(spans):
                af[s, :] = out[i * rows : (i + 1) * rows]
                df[s, :] = grad_query[i * rows : (i + 1) * rows]
            key_terms = nn(grad_scores, query)
            value_terms = nn(probs, grad)
            if pair == 0:
                sums[0] = key_terms
                sums[1] = value_terms
            else:
                sums[0] += key_terms
                sums[1] += value_terms
        for which, factor in ((0, scale), (1, 1.0)):
            own_ref[which, kv] = sums[which, :rows] * factor
            for i in range(1, listed):
                term = sums[which, i * rows : (i + 1) * rows] * factor
                block = chosen_ref[i]
                terms_ref[block, which, kv] = (
                    terms_ref[block, which, kv].astype(FLOAT) + term
                ).astype(HALF)
        return 0

    lax.fori_loop(0, kv_count, group, 0)
    att_ref[...] = af[...].astype(HALF)
    dq_ref[...] = df[...].astype(HALF)


def attend(chosen, query_rows, grad_rows, fetched):
    total, width = query_rows.shape
    _, _, kv_count, rows, _ = fetched.shape
    listed = chosen.shape[0]
    whole = pl.BlockSpec(memory_space=pltpu.VMEM)
    return pl.pallas_call(
        attend_kernel,
        out_shape=(
            jax.ShapeDtypeStruct((total, width), HALF),
            jax.ShapeDtypeStruct((total, width), HALF),
            jax.ShapeDtypeStruct((2, kv_count, rows, width), FLOAT),
            jax.ShapeDtypeStruct(fetched.shape, HALF),
        ),
        in_specs=[pl.BlockSpec(memory_space=pltpu.SMEM), whole, whole, whole],
        out_specs=(whole,) * 4,
        scratch_shapes=[pltpu.VMEM((total, width), FLOAT)] * 4
        + [pltpu.VMEM((2, listed * rows, width), FLOAT)],
        compiler_params=pltpu.CompilerParams(vmem_limit_bytes=48 * 2**20),
    )(chosen, query_rows, grad_rows, fetched)


def pick(codes, z):
    packed = sum(code * 4**i for i, code in enumerate(codes))
    return packed // ((1 + 3 * (z % 2)) * (1 + 15 * (z // 2))) % 4


ORDER = ((3, 3, 0, 0), (2, 0, 3, 1), (1, 2, 1, 2), (0, 1, 2, 3))


def scatter_kernel(
    terms_ref, own_ref, out_ref,
    from_core, from_side, from_up, from_down, to_side, to_row, acc,
    core_send, side_send, row_send, core_recv, side_recv, up_recv, down_recv,
):
    me, z, x, c = place()
    sibling, across, up, down = neighbours(me, z, x, c)

    def copy(src, dst, send, recv, target):
        return pltpu.make_async_remote_copy(
            src_ref=src, dst_ref=dst, send_sem=send, recv_sem=recv,
            device_id={"seq": target}, device_id_type=MESH,
        )

    def core_copy(row, col, half):
        return copy(
            terms_ref.at[row * 4 + col * 2 + 1 - c, half], from_core.at[row, col, half],
            core_send.at[row, col, half], core_recv.at[row, col, half], sibling,
        )

    def side_copy(row, half):
        return copy(
            to_side.at[row, half], from_side.at[row, half],
            side_send.at[row, half], side_recv.at[row, half], across,
        )

    def up_copy(row, half):
        return copy(
            to_row.at[row, half], from_down.at[row, half],
            row_send.at[row, half], down_recv.at[row, half], up,
        )

    def down_copy(row, half):
        return copy(
            to_row.at[row, half], from_up.at[row, half],
            row_send.at[row, half], up_recv.at[row, half], down,
        )

    greet(me, z, x, c)
    rows = [pick(codes, z) for codes in ORDER]
    for row in rows:
        for half in range(2):
            core_copy(row, 1 - x, half).start()
    for row in rows:
        for half in range(2):
            core_copy(row, x, half).start()
    for row in rows:
        for half in range(2):
            core_copy(row, 1 - x, half).wait_recv()
            to_side[row, half] = (
                terms_ref[row * 4 + (1 - x) * 2 + c, half].astype(FLOAT)
                + from_core[row, 1 - x, half].astype(FLOAT)
            ).astype(HALF)
            side_copy(row, half).start()
    for step, row in enumerate(rows):
        for half in range(2):
            core_copy(row, x, half).wait_recv()
            side_copy(row, half).wait_recv()
            acc[...] = (
                terms_ref[row * 4 + x * 2 + c, half].astype(FLOAT)
                + from_core[row, x, half].astype(FLOAT)
                + from_side[row, half].astype(FLOAT)
            )

            @pl.when((row >= z) & (z > 0))
            def _(row=row, half=half):
                up_copy(row, half).wait_recv()
                acc[...] += from_down[row, half].astype(FLOAT)

            @pl.when((row <= z) & (z < FAR - 1))
            def _(row=row, half=half):
                down_copy(row, half).wait_recv()
                acc[...] += from_up[row, half].astype(FLOAT)

            if step < FAR - 1:
                to_row[row, half] = acc[...].astype(HALF)

                @pl.when(row > z)
                def _(row=row, half=half):
                    up_copy(row, half).start()

                @pl.when(row < z)
                def _(row=row, half=half):
                    down_copy(row, half).start()
            else:
                out_ref[half] = (acc[...] + own_ref[half]).astype(HALF)
    for step, row in enumerate(rows):
        for half in range(2):
            side_copy(row, half).wait_send()
            for col in range(SIDE):
                core_copy(row, col, half).wait_send()
            if step < FAR - 1:
                up_copy(row, half).wait_send()


def scatter(terms, own):
    tile = own.shape[1:]
    dma = pltpu.SemaphoreType.DMA
    whole = pl.BlockSpec(memory_space=pltpu.VMEM)
    slots = pltpu.VMEM((FAR, 2, *tile), HALF)
    return pl.pallas_call(
        scatter_kernel,
        out_shape=jax.ShapeDtypeStruct(own.shape, HALF),
        in_specs=[whole, whole],
        out_specs=whole,
        scratch_shapes=[
            pltpu.VMEM((FAR, SIDE, 2, *tile), HALF),
            slots, slots, slots, slots, slots,
            pltpu.VMEM(tile, FLOAT),
            dma((FAR, SIDE, 2)), dma((FAR, 2)), dma((FAR, 2)),
            dma((FAR, SIDE, 2)), dma((FAR, 2)), dma((FAR, 2)), dma((FAR, 2)),
        ],
        compiler_params=pltpu.CompilerParams(
            collective_id=1, has_side_effects=True, vmem_limit_bytes=40 * 2**20
        ),
    )(terms, own)


def local(queries, key_heads, value_heads, grad_out, offsets, random_masks, global_blocks):
    rows, heads, width = queries.shape
    me = lax.axis_index("seq").astype(jnp.int32)
    chosen = jnp.concatenate([me[None], me ^ offsets, me ^ random_masks, global_blocks])
    kv = jnp.stack([key_heads, value_heads]).transpose(0, 2, 1, 3)
    fetched = gather(kv)
    attended, grad_queries, own, terms = attend(
        chosen, queries.reshape(rows * heads, width), grad_out.reshape(rows * heads, width), fetched
    )
    totals = scatter(terms, own).transpose(0, 2, 1, 3)
    return (
        attended.reshape(queries.shape), grad_queries.reshape(queries.shape), totals[0], totals[1]
    )


def solution(mesh):
    return jax.shard_map(
        local if mesh.shape["seq"] == FAR * SIDE * CORES else local_any,
        mesh=mesh,
        in_specs=(
            P(("groups", "seq"), None, None),
            P(("groups", "seq"), None, None),
            P(("groups", "seq"), None, None),
            P(("groups", "seq"), None, None),
            P(),
            P(),
            P(),
        ),
        out_specs=(
            P(("groups", "seq"), None, None),
            P(("groups", "seq"), None, None),
            P(("groups", "seq"), None, None),
            P(("groups", "seq"), None, None),
        ),
        check_vma=False,
    )
```

```python
import jax
import jax.numpy as jnp
from jax import lax
from jax.experimental import pallas as pl
from jax.experimental.pallas import tpu as pltpu
from jax.sharding import PartitionSpec as P


def from_partner(x, axis, distance):
    return lax.ppermute(x, axis, [(i, i ^ 1 << distance) for i in range(lax.axis_size(axis))])


def broadcast(value, axis, source):
    kept = jnp.where(lax.axis_index(axis) == source, value, 0).astype(value.dtype)
    return lax.psum(kept, axis)


def forward_head(inputs):
    query_part, key_part, value_part = inputs
    scale = query_part.shape[-1] ** (-0.5)
    scores = (
        jnp.einsum("qpd,kd->pqk", query_part, key_part, preferred_element_type=jnp.float32) * scale
    )
    top_score = jnp.max(scores, axis=-1, keepdims=True)
    log_total = top_score[..., 0] + jnp.log(jnp.sum(jnp.exp(scores - top_score), axis=-1))
    probs = jnp.exp(scores - log_total[..., None]).astype(jnp.bfloat16)
    output_part = jnp.einsum("pqk,kd->qpd", probs, value_part, preferred_element_type=jnp.float32)
    return (output_part.astype(jnp.bfloat16), log_total)


def backward_head(inputs):
    query_part, key_part, value_part, grad_part, output_part, log_total = inputs
    scale = query_part.shape[-1] ** (-0.5)
    scores = (
        jnp.einsum("qpd,kd->pqk", query_part, key_part, preferred_element_type=jnp.float32) * scale
    )
    weights = jnp.exp(scores - log_total[..., None])
    probs = weights.astype(jnp.bfloat16)
    deltas = jnp.sum(grad_part.astype(jnp.float32) * output_part.astype(jnp.float32), axis=-1).T
    value_terms = jnp.einsum("pqk,qpd->kd", probs, grad_part, preferred_element_type=jnp.float32)
    grad_probs = jnp.einsum(
        "qpd,kd->pqk", grad_part, value_part, preferred_element_type=jnp.float32
    )
    grad_scores = (weights * (grad_probs - deltas[..., None])).astype(jnp.bfloat16)
    grad_query = (
        jnp.einsum("pqk,kd->qpd", grad_scores, key_part, preferred_element_type=jnp.float32) * scale
    )
    key_terms = (
        jnp.einsum("pqk,qpd->kd", grad_scores, query_part, preferred_element_type=jnp.float32)
        * scale
    )
    return (grad_query.astype(jnp.bfloat16), key_terms, value_terms)


def kv_hop(tensor, bit_number):
    return from_partner(tensor, "seq", bit_number)


def grad_hop(tensor, bit_number):
    return from_partner(tensor.astype(jnp.bfloat16), "seq", bit_number).astype(tensor.dtype)


def bit_sequence():
    width_bits = lax.axis_size("seq").bit_length() - 1
    return list(range(width_bits))


def route(tensor, distance, hop):
    for bit_number in bit_sequence():
        tensor = lax.cond(
            jnp.bitwise_and(jnp.right_shift(distance, bit_number), 1) == 1,
            lambda moved, bit_number=bit_number: hop(moved, bit_number),
            lambda moved: moved,
            tensor,
        )
    return tensor


def fetch_blocks(stacked, distances, global_blocks):
    fetched = [stacked]
    for position in range(distances.shape[0]):
        fetched.append(route(stacked, distances[position], kv_hop))
    position = 0
    fetched.append(broadcast(stacked, "seq", global_blocks[position]))
    return jnp.stack(fetched)


def head_major(fetched, which):
    listed, rows, kv_count, width = (
        fetched.shape[0],
        fetched.shape[2],
        fetched.shape[3],
        fetched.shape[4],
    )
    return fetched[:, which].reshape(listed * rows, kv_count, width).transpose(1, 0, 2)


def local_any(queries, key_heads, value_heads, grad_out, offsets, random_masks, global_blocks):
    rows, heads, width = queries.shape
    kv_count = key_heads.shape[1]
    grouped = heads // kv_count
    distances = jnp.concatenate([offsets, random_masks])
    routed_count = distances.shape[0]
    stacked = jnp.stack([key_heads, value_heads])
    query_part = queries.reshape(rows, kv_count, grouped, width).transpose(1, 0, 2, 3)
    grad_part = grad_out.reshape(rows, kv_count, grouped, width).transpose(1, 0, 2, 3)
    fetched = fetch_blocks(stacked, distances, global_blocks)
    output_part, log_total = lax.map(
        forward_head, (query_part, head_major(fetched, 0), head_major(fetched, 1))
    )
    listed = fetched.shape[0]
    grad_query, key_terms, value_terms = lax.map(
        backward_head,
        (
            query_part,
            head_major(fetched, 0),
            head_major(fetched, 1),
            grad_part,
            output_part,
            log_total,
        ),
    )
    terms = (
        jnp.stack([key_terms, value_terms])
        .reshape(2, kv_count, listed, rows, width)
        .transpose(2, 0, 3, 1, 4)
    )
    totals = terms[0]
    for position in range(routed_count):
        totals = totals + route(terms[1 + position], distances[position], grad_hop)
    summed = lax.psum(terms[1 + routed_count :], "seq")
    owner = lax.axis_index("seq")
    position = 0
    totals = totals + jnp.where(
        owner == global_blocks[position], summed[position], jnp.float32(0.0)
    )
    attended = output_part.transpose(1, 0, 2, 3).reshape(rows, heads, width)
    grad_queries = grad_query.transpose(1, 0, 2, 3).reshape(rows, heads, width)
    grad_keys = totals[0].astype(jnp.bfloat16)
    grad_values = totals[1].astype(jnp.bfloat16)
    return (attended, grad_queries, grad_keys, grad_values)


MESH = pl.DeviceIdType.MESH
FLOAT = jnp.float32
HALF = jnp.bfloat16
FAR, SIDE, CORES = 4, 2, 2


def place():
    me = lax.axis_index("seq")
    return me, me // 4, (me // 2) % 2, me % 2


def neighbours(me, z, x, c):
    sibling = me + 1 - 2 * c
    across = me + 2 - 4 * x
    return sibling, across, me + 4, me - 4


def greet(me, z, x, c):
    sibling, across, up, down = neighbours(me, z, x, c)
    barrier = pltpu.get_barrier_semaphore()
    for other in (sibling, across):
        pl.semaphore_signal(barrier, inc=1, device_id={"seq": other}, device_id_type=MESH)

    @pl.when(z < FAR - 1)
    def _():
        pl.semaphore_signal(barrier, inc=1, device_id={"seq": up}, device_id_type=MESH)

    @pl.when(z > 0)
    def _():
        pl.semaphore_signal(barrier, inc=1, device_id={"seq": down}, device_id_type=MESH)

    pl.semaphore_wait(barrier, 3 + (z + 1) // 2 % 2)


def nt(a, b):
    return lax.dot_general(a, b, (((1,), (1,)), ((), ())), preferred_element_type=FLOAT)


def nn(a, b):
    return lax.dot_general(a, b, (((1,), (0,)), ((), ())), preferred_element_type=FLOAT)


def pick(codes, z):
    packed = sum(code * 4**i for i, code in enumerate(codes))
    return packed // ((1 + 3 * (z % 2)) * (1 + 15 * (z // 2))) % 4


ORDER = ((3, 3, 0, 0), (2, 0, 3, 1), (1, 2, 1, 2), (0, 1, 2, 3))


def layer_kernel(
    chosen_ref, named_ref, q_ref, g_ref, kv_ref,
    att_ref, dq_ref, out_ref,
    qf, gf, af, df, sums, merged, all_first, all_second, own, keep, give,
    from_core, from_side, from_up, from_down, to_side, to_row, acc,
    own_sem, gather_side, gather_core, gather_up, gather_down, gather_recv,
    core_send, side_send, row_send, core_recv, side_recv, up_recv, down_recv,
):
    me, z, x, c = place()
    sibling, across, up, down = neighbours(me, z, x, c)
    blocks = (all_first, all_second)
    listed = chosen_ref.shape[0]
    _, _, per_half, rows, width = kv_ref.shape
    heads = q_ref.shape[0] // rows
    grouped = heads // (2 * per_half)
    pairs = grouped // 2
    scale = width ** (-0.5)

    def remote(src, dst, send, recv, target):
        return pltpu.make_async_remote_copy(
            src_ref=src, dst_ref=dst, send_sem=send, recv_sem=recv,
            device_id={"seq": target}, device_id_type=MESH,
        )

    def copy(slot, half, sem, target, mine=False):
        return remote(
            kv_ref.at[half] if mine else blocks[half].at[slot], blocks[half].at[slot],
            sem, gather_recv.at[slot, half], target,
        )

    def column(row):
        return row * 4 + x * 2 + c

    def opposite(row):
        return row * 4 + (1 - x) * 2 + c

    def arrived(slot, half):
        copy(slot, half, gather_side.at[0, half], across).wait_recv()

    def pass_on(row, half, upward, downward, mine=False):
        slot = column(row)
        copy(slot, half, gather_side.at[row, half], across, mine).start()
        if upward:

            @pl.when(z < FAR - 1)
            def _():
                copy(slot, half, gather_up.at[row, half], up, mine).start()

        if downward:

            @pl.when(z > 0)
            def _():
                copy(slot, half, gather_down.at[row, half], down, mine).start()

        copy(slot, half, gather_core.at[0, row, half], sibling, mine).start()

    def own_copy(half):
        return pltpu.make_async_copy(kv_ref.at[half], blocks[half].at[me], own_sem.at[half])

    def gather_start(half):
        pass_on(z, half, True, True, mine=True)
        own_copy(half).start()

    def share(row, half):
        arrived(opposite(row), half)
        copy(opposite(row), half, gather_core.at[1, row, half], sibling).start()

    def gather_shares(step, half):
        if step == 0:
            share(z, half)
            return

        @pl.when(z - step >= 0)
        def _():
            share(z - step, half)

        @pl.when(z + step < FAR)
        def _():
            share(z + step, half)

    def gather_step(step, half):
        @pl.when(z - step >= 0)
        def _():
            arrived(column(z - step), half)
            pass_on(z - step, half, True, False)

        @pl.when(z + step < FAR)
        def _():
            arrived(column(z + step), half)
            pass_on(z + step, half, False, True)

    def gather_end(half):
        for row in range(FAR):
            for col in range(SIDE):
                arrived(row * 4 + col * 2 + 1 - c, half)
        own_copy(half).wait()

    def gather_sent(half):
        for row in range(FAR):
            copy(column(row), half, gather_side.at[row, half], across).wait_send()
            for which in range(2):
                copy(column(row), half, gather_core.at[which, row, half], sibling).wait_send()

            @pl.when((z < FAR - 1) & (z >= row))
            def _(row=row):
                copy(column(row), half, gather_up.at[row, half], up).wait_send()

            @pl.when((z > 0) & (z <= row))
            def _(row=row):
                copy(column(row), half, gather_down.at[row, half], down).wait_send()

    def attend(half, between):
        fetched = blocks[half]

        def one(head, _):
            keys = jnp.concatenate([fetched[chosen_ref[i], 0, head] for i in range(listed)], axis=0)
            values = jnp.concatenate(
                [fetched[chosen_ref[i], 1, head] for i in range(listed)], axis=0
            )
            keys_t, values_t = keys.T, values.T
            for pair in range(pairs):
                first = (half * per_half + head) * grouped + 2 * pair
                spans = [pl.ds(first + i, rows, stride=heads) for i in range(2)]
                query = jnp.concatenate([qf[s, :] for s in spans], axis=0).astype(HALF)
                grad = jnp.concatenate([gf[s, :] for s in spans], axis=0).astype(HALF)
                scores = nt(keys, query)
                top = jnp.max(scores, axis=0, keepdims=True)
                weights = jnp.exp((scores - top) * scale)
                weights = weights * (1.0 / jnp.sum(weights, axis=0, keepdims=True))
                probs = weights.astype(HALF)
                out = nn(values_t, probs).T
                grad_probs = nt(values, grad)
                deltas = jnp.sum(weights * grad_probs, axis=0, keepdims=True)
                grad_scores = (weights * (grad_probs - deltas)).astype(HALF)
                grad_query = (nn(keys_t, grad_scores) * scale).T
                for i, s in enumerate(spans):
                    af[s, :] = out[i * rows : (i + 1) * rows]
                    df[s, :] = grad_query[i * rows : (i + 1) * rows]
                key_terms = nn(grad_scores, query).reshape(listed, rows, width)
                value_terms = nn(probs, grad).reshape(listed, rows, width)
                if pair == 0:
                    sums[:, 0] = key_terms
                    sums[:, 1] = value_terms
                else:
                    sums[:, 0] += key_terms
                    sums[:, 1] += value_terms
                between(head, pair)
            for which, factor in ((0, scale), (1, 1.0)):
                own[half, which, head] = sums[0, which] * factor
                for i in range(1, listed):
                    total = sums[i, which]
                    for j in range(1, listed):
                        if j != i:
                            same = chosen_ref[j] == chosen_ref[i]
                            total = total + jnp.where(same, sums[j, which], 0.0)
                    merged[i, which] = total * factor
                merged[0, which] = jnp.zeros((rows, width), FLOAT)
            for row in range(FAR):
                for col in range(SIDE):
                    slot = row * 4 + col * 2
                    keep[half, row, col, :, head] = merged[named_ref[slot + c]]
                    give[half, row, col, :, head] = merged[named_ref[slot + 1 - c]].astype(HALF)
            return 0

        lax.fori_loop(0, per_half, one, 0)

    def core_copy(row, col, half):
        return remote(
            give.at[half, row, col], from_core.at[half, row, col],
            core_send.at[half, row, col], core_recv.at[half, row, col], sibling,
        )

    def side_copy(row, half):
        return remote(
            to_side.at[half, row], from_side.at[half, row],
            side_send.at[half, row], side_recv.at[half, row], across,
        )

    def up_copy(row, half):
        return remote(
            to_row.at[half, row], from_down.at[half, row],
            row_send.at[half, row], down_recv.at[half, row], up,
        )

    def down_copy(row, half):
        return remote(
            to_row.at[half, row], from_up.at[half, row],
            row_send.at[half, row], up_recv.at[half, row], down,
        )

    order = [pick(codes, z) for codes in ORDER]

    def core_start(half):
        for row in order:
            core_copy(row, 1 - x, half).start()
        for row in order:
            core_copy(row, x, half).start()

    def side_step(step, half):
        row = order[step]
        core_copy(row, 1 - x, half).wait_recv()
        to_side[half, row] = (
            keep[half, row, 1 - x] + from_core[half, row, 1 - x].astype(FLOAT)
        ).astype(HALF)
        side_copy(row, half).start()

    def row_step(step, half):
        row = order[step]
        core_copy(row, x, half).wait_recv()
        side_copy(row, half).wait_recv()
        acc[...] = (
            keep[half, row, x]
            + from_core[half, row, x].astype(FLOAT)
            + from_side[half, row].astype(FLOAT)
        )

        @pl.when((row >= z) & (z > 0))
        def _():
            up_copy(row, half).wait_recv()
            acc[...] += from_down[half, row].astype(FLOAT)

        @pl.when((row <= z) & (z < FAR - 1))
        def _():
            down_copy(row, half).wait_recv()
            acc[...] += from_up[half, row].astype(FLOAT)

        if step < FAR - 1:
            to_row[half, row] = acc[...].astype(HALF)

            @pl.when(row > z)
            def _():
                up_copy(row, half).start()

            @pl.when(row < z)
            def _():
                down_copy(row, half).start()
        else:
            out_ref[half] = (acc[...] + own[half]).astype(HALF)

    def sum_sent(half):
        for step, row in enumerate(order):
            side_copy(row, half).wait_send()
            for col in range(SIDE):
                core_copy(row, col, half).wait_send()
            if step < FAR - 1:
                up_copy(row, half).wait_send()

    def schedule(actions):
        def between(head, pair):
            for (at_head, at_pair), action in actions.items():
                if at_pair == pair:
                    pl.when(head == at_head)(action)

        return between

    def during_first_a():
        gather_step(3, 1)
        gather_shares(0, 1)

    def during_first_b():
        gather_shares(1, 1)

    def during_first_c():
        gather_shares(2, 1)

    def during_first_d():
        gather_shares(3, 1)

    def during_second_a():
        side_step(0, 0)
        side_step(1, 0)

    def during_second_b():
        side_step(2, 0)
        side_step(3, 0)

    greet(me, z, x, c)
    gather_start(0)
    gf[...] = g_ref[...].astype(FLOAT)
    gather_step(1, 0)
    gather_step(2, 0)
    gather_start(1)
    qf[...] = q_ref[...].astype(FLOAT)
    gather_shares(0, 0)
    gather_step(3, 0)
    gather_shares(1, 0)
    gather_step(1, 1)
    gather_shares(2, 0)
    gather_step(2, 1)
    gather_shares(3, 0)
    gather_end(0)
    attend(
        0,
        schedule(
            {
                (0, 0): during_first_a,
                (0, 1): during_first_b,
                (1, 0): during_first_c,
                (1, 1): during_first_d,
            }
        ),
    )
    core_start(0)
    gather_end(1)
    attend(
        1,
        schedule(
            {
                (0, 0): during_second_a,
                (0, 1): during_second_b,
                (1, 0): lambda: row_step(0, 0),
                (1, 1): lambda: row_step(1, 0),
                (1, 2): lambda: row_step(2, 0),
            }
        ),
    )
    core_start(1)
    for step in range(FAR):
        side_step(step, 1)
    row_step(3, 0)
    att_ref[...] = af[...].astype(HALF)
    dq_ref[...] = df[...].astype(HALF)
    for step in range(FAR):
        row_step(step, 1)
    for half in range(2):
        gather_sent(half)
        sum_sent(half)


def layer(chosen, named, query_rows, grad_rows, kv):
    total, width = query_rows.shape
    _, _, per_half, rows, _ = kv.shape
    listed = chosen.shape[0]
    tile = kv.shape[1:]
    dma = pltpu.SemaphoreType.DMA
    whole = pl.BlockSpec(memory_space=pltpu.VMEM)
    scalars = pl.BlockSpec(memory_space=pltpu.SMEM)
    slots = pltpu.VMEM((2, FAR, *tile), HALF)
    long = pltpu.VMEM((total, width), FLOAT)
    fetched = pltpu.VMEM((FAR * SIDE * CORES, *tile), HALF)
    by_slot = (2, FAR, SIDE)
    return pl.pallas_call(
        layer_kernel,
        out_shape=(
            jax.ShapeDtypeStruct((total, width), HALF),
            jax.ShapeDtypeStruct((total, width), HALF),
            jax.ShapeDtypeStruct(kv.shape, HALF),
        ),
        in_specs=[scalars, scalars, whole, whole, whole],
        out_specs=(whole,) * 3,
        scratch_shapes=[
            long, long, long, long,
            pltpu.VMEM((listed, 2, rows, width), FLOAT),
            pltpu.VMEM((listed, 2, rows, width), FLOAT),
            fetched, fetched,
            pltpu.VMEM(kv.shape, FLOAT),
            pltpu.VMEM((*by_slot, *tile), FLOAT),
            pltpu.VMEM((*by_slot, *tile), HALF),
            pltpu.VMEM((*by_slot, *tile), HALF),
            slots, slots, slots, slots, slots,
            pltpu.VMEM(tile, FLOAT),
            dma((2,)), dma((FAR, 2)), dma((2, FAR, 2)), dma((FAR, 2)), dma((FAR, 2)),
            dma((FAR * SIDE * CORES, 2)),
            dma(by_slot), dma((2, FAR)), dma((2, FAR)),
            dma(by_slot), dma((2, FAR)), dma((2, FAR)), dma((2, FAR)),
        ],
        compiler_params=pltpu.CompilerParams(
            collective_id=0, has_side_effects=True, vmem_limit_bytes=56 * 2**20
        ),
    )(chosen, named, query_rows, grad_rows, kv)


def local(queries, key_heads, value_heads, grad_out, offsets, random_masks, global_blocks):
    rows, heads, width = queries.shape
    kv_count = key_heads.shape[1]
    me = lax.axis_index("seq").astype(jnp.int32)
    chosen = jnp.concatenate([me[None], me ^ offsets, me ^ random_masks, global_blocks])
    slots = jnp.arange(FAR * SIDE * CORES, dtype=jnp.int32)
    named = jnp.zeros_like(slots)
    for i in range(1, chosen.shape[0]):
        named = jnp.where(slots == chosen[i], i, named)
    kv = jnp.stack([key_heads, value_heads]).reshape(2, rows, 2, kv_count // 2, width)
    attended, grad_queries, totals = layer(
        chosen, named,
        queries.reshape(rows * heads, width), grad_out.reshape(rows * heads, width),
        kv.transpose(2, 0, 3, 1, 4),
    )
    totals = totals.transpose(1, 3, 0, 2, 4).reshape(2, rows, kv_count, width)
    return (
        attended.reshape(queries.shape), grad_queries.reshape(queries.shape), totals[0], totals[1]
    )


def solution(mesh):
    return jax.shard_map(
        local if mesh.shape["seq"] == FAR * SIDE * CORES else local_any,
        mesh=mesh,
        in_specs=(
            P(("groups", "seq"), None, None),
            P(("groups", "seq"), None, None),
            P(("groups", "seq"), None, None),
            P(("groups", "seq"), None, None),
            P(),
            P(),
            P(),
        ),
        out_specs=(
            P(("groups", "seq"), None, None),
            P(("groups", "seq"), None, None),
            P(("groups", "seq"), None, None),
            P(("groups", "seq"), None, None),
        ),
        check_vma=False,
    )
```

```python
import jax
import jax.numpy as jnp
from jax import lax
from jax.experimental import pallas as pl
from jax.experimental.pallas import tpu as pltpu
from jax.sharding import PartitionSpec as P


def from_partner(x, axis, distance):
    return lax.ppermute(x, axis, [(i, i ^ 1 << distance) for i in range(lax.axis_size(axis))])


def broadcast(value, axis, source):
    kept = jnp.where(lax.axis_index(axis) == source, value, 0).astype(value.dtype)
    return lax.psum(kept, axis)


def forward_head(inputs):
    query_part, key_part, value_part = inputs
    scale = query_part.shape[-1] ** (-0.5)
    scores = (
        jnp.einsum("qpd,kd->pqk", query_part, key_part, preferred_element_type=jnp.float32) * scale
    )
    top_score = jnp.max(scores, axis=-1, keepdims=True)
    log_total = top_score[..., 0] + jnp.log(jnp.sum(jnp.exp(scores - top_score), axis=-1))
    probs = jnp.exp(scores - log_total[..., None]).astype(jnp.bfloat16)
    output_part = jnp.einsum("pqk,kd->qpd", probs, value_part, preferred_element_type=jnp.float32)
    return (output_part.astype(jnp.bfloat16), log_total)


def backward_head(inputs):
    query_part, key_part, value_part, grad_part, output_part, log_total = inputs
    scale = query_part.shape[-1] ** (-0.5)
    scores = (
        jnp.einsum("qpd,kd->pqk", query_part, key_part, preferred_element_type=jnp.float32) * scale
    )
    weights = jnp.exp(scores - log_total[..., None])
    probs = weights.astype(jnp.bfloat16)
    deltas = jnp.sum(grad_part.astype(jnp.float32) * output_part.astype(jnp.float32), axis=-1).T
    value_terms = jnp.einsum("pqk,qpd->kd", probs, grad_part, preferred_element_type=jnp.float32)
    grad_probs = jnp.einsum(
        "qpd,kd->pqk", grad_part, value_part, preferred_element_type=jnp.float32
    )
    grad_scores = (weights * (grad_probs - deltas[..., None])).astype(jnp.bfloat16)
    grad_query = (
        jnp.einsum("pqk,kd->qpd", grad_scores, key_part, preferred_element_type=jnp.float32) * scale
    )
    key_terms = (
        jnp.einsum("pqk,qpd->kd", grad_scores, query_part, preferred_element_type=jnp.float32)
        * scale
    )
    return (grad_query.astype(jnp.bfloat16), key_terms, value_terms)


def kv_hop(tensor, bit_number):
    return from_partner(tensor, "seq", bit_number)


def grad_hop(tensor, bit_number):
    return from_partner(tensor.astype(jnp.bfloat16), "seq", bit_number).astype(tensor.dtype)


def bit_sequence():
    width_bits = lax.axis_size("seq").bit_length() - 1
    return list(range(width_bits))


def route(tensor, distance, hop):
    for bit_number in bit_sequence():
        tensor = lax.cond(
            jnp.bitwise_and(jnp.right_shift(distance, bit_number), 1) == 1,
            lambda moved, bit_number=bit_number: hop(moved, bit_number),
            lambda moved: moved,
            tensor,
        )
    return tensor


def fetch_blocks(stacked, distances, global_blocks):
    fetched = [stacked]
    for position in range(distances.shape[0]):
        fetched.append(route(stacked, distances[position], kv_hop))
    position = 0
    fetched.append(broadcast(stacked, "seq", global_blocks[position]))
    return jnp.stack(fetched)


def head_major(fetched, which):
    listed, rows, kv_count, width = (
        fetched.shape[0],
        fetched.shape[2],
        fetched.shape[3],
        fetched.shape[4],
    )
    return fetched[:, which].reshape(listed * rows, kv_count, width).transpose(1, 0, 2)


def local_any(queries, key_heads, value_heads, grad_out, offsets, random_masks, global_blocks):
    rows, heads, width = queries.shape
    kv_count = key_heads.shape[1]
    grouped = heads // kv_count
    distances = jnp.concatenate([offsets, random_masks])
    routed_count = distances.shape[0]
    stacked = jnp.stack([key_heads, value_heads])
    query_part = queries.reshape(rows, kv_count, grouped, width).transpose(1, 0, 2, 3)
    grad_part = grad_out.reshape(rows, kv_count, grouped, width).transpose(1, 0, 2, 3)
    fetched = fetch_blocks(stacked, distances, global_blocks)
    output_part, log_total = lax.map(
        forward_head, (query_part, head_major(fetched, 0), head_major(fetched, 1))
    )
    listed = fetched.shape[0]
    grad_query, key_terms, value_terms = lax.map(
        backward_head,
        (
            query_part,
            head_major(fetched, 0),
            head_major(fetched, 1),
            grad_part,
            output_part,
            log_total,
        ),
    )
    terms = (
        jnp.stack([key_terms, value_terms])
        .reshape(2, kv_count, listed, rows, width)
        .transpose(2, 0, 3, 1, 4)
    )
    totals = terms[0]
    for position in range(routed_count):
        totals = totals + route(terms[1 + position], distances[position], grad_hop)
    summed = lax.psum(terms[1 + routed_count :], "seq")
    owner = lax.axis_index("seq")
    position = 0
    totals = totals + jnp.where(
        owner == global_blocks[position], summed[position], jnp.float32(0.0)
    )
    attended = output_part.transpose(1, 0, 2, 3).reshape(rows, heads, width)
    grad_queries = grad_query.transpose(1, 0, 2, 3).reshape(rows, heads, width)
    grad_keys = totals[0].astype(jnp.bfloat16)
    grad_values = totals[1].astype(jnp.bfloat16)
    return (attended, grad_queries, grad_keys, grad_values)


MESH = pl.DeviceIdType.MESH
FLOAT = jnp.float32
HALF = jnp.bfloat16
FAR, SIDE, CORES = 4, 2, 2


def place():
    me = lax.axis_index("seq")
    return me, me // 4, (me // 2) % 2, me % 2


def neighbours(me, z, x, c):
    sibling = me + 1 - 2 * c
    across = me + 2 - 4 * x
    return sibling, across, me + 4, me - 4


def greet(me, z, x, c):
    sibling, across, up, down = neighbours(me, z, x, c)
    barrier = pltpu.get_barrier_semaphore()
    for other in (sibling, across):
        pl.semaphore_signal(barrier, inc=1, device_id={"seq": other}, device_id_type=MESH)

    @pl.when(z < FAR - 1)
    def _():
        pl.semaphore_signal(barrier, inc=1, device_id={"seq": up}, device_id_type=MESH)

    @pl.when(z > 0)
    def _():
        pl.semaphore_signal(barrier, inc=1, device_id={"seq": down}, device_id_type=MESH)

    pl.semaphore_wait(barrier, 3 + (z + 1) // 2 % 2)


def nt(a, b):
    return lax.dot_general(a, b, (((1,), (1,)), ((), ())), preferred_element_type=FLOAT)


def nn(a, b):
    return lax.dot_general(a, b, (((1,), (0,)), ((), ())), preferred_element_type=FLOAT)


def pick(codes, z):
    packed = sum(code * 4**i for i, code in enumerate(codes))
    return packed // ((1 + 3 * (z % 2)) * (1 + 15 * (z // 2))) % 4


ORDER = ((3, 3, 0, 0), (2, 0, 3, 1), (1, 2, 1, 2), (0, 1, 2, 3))


def layer_kernel(
    offsets_ref, masks_ref, globals_ref, q_ref, g_ref, kv_ref,
    att_ref, dq_ref, dk_ref, dv_ref,
    qf, gf, af, df, sums, merged, all_0, all_1, all_2, all_3, own, keep, give,
    from_core, from_side, from_up, from_down, to_side, to_row, acc,
    own_sem, gather_side, gather_core, gather_up, gather_down, gather_recv,
    core_send, side_send, row_send, core_recv, side_recv, up_recv, down_recv,
):
    me, z, x, c = place()
    sibling, across, up, down = neighbours(me, z, x, c)
    blocks = (all_0, all_1, all_2, all_3)
    chosen = [me]
    chosen += [me ^ offsets_ref[i] for i in range(offsets_ref.shape[0])]
    chosen += [me ^ masks_ref[i] for i in range(masks_ref.shape[0])]
    chosen += [globals_ref[i] for i in range(globals_ref.shape[0])]
    listed = len(chosen)
    parts, _, rows, width = kv_ref.shape
    heads = q_ref.shape[0] // rows
    grouped = heads // parts
    pairs = grouped // 2
    scale = width ** (-0.5)

    def remote(src, dst, send, recv, target):
        return pltpu.make_async_remote_copy(
            src_ref=src, dst_ref=dst, send_sem=send, recv_sem=recv,
            device_id={"seq": target}, device_id_type=MESH,
        )

    def copy(slot, part, sem, target, mine=False):
        return remote(
            kv_ref.at[part] if mine else blocks[part].at[slot], blocks[part].at[slot],
            sem, gather_recv.at[slot, part], target,
        )

    def column(row):
        return row * 4 + x * 2 + c

    def opposite(row):
        return row * 4 + (1 - x) * 2 + c

    def arrived(slot, part):
        copy(slot, part, gather_side.at[0, part], across).wait_recv()

    def pass_on(row, part, upward, downward, mine=False):
        slot = column(row)
        copy(slot, part, gather_side.at[row, part], across, mine).start()
        if upward:

            @pl.when(z < FAR - 1)
            def _():
                copy(slot, part, gather_up.at[row, part], up, mine).start()

        if downward:

            @pl.when(z > 0)
            def _():
                copy(slot, part, gather_down.at[row, part], down, mine).start()

        copy(slot, part, gather_core.at[0, row, part], sibling, mine).start()

    def own_copy(part):
        return pltpu.make_async_copy(kv_ref.at[part], blocks[part].at[me], own_sem.at[part])

    def gather_start(part):
        pass_on(z, part, True, True, mine=True)
        own_copy(part).start()

    def share(row, part):
        arrived(opposite(row), part)
        copy(opposite(row), part, gather_core.at[1, row, part], sibling).start()

    def gather_shares(step, part):
        if step == 0:
            share(z, part)
            return

        @pl.when(z - step >= 0)
        def _():
            share(z - step, part)

        @pl.when(z + step < FAR)
        def _():
            share(z + step, part)

    def gather_step(step, part):
        @pl.when(z - step >= 0)
        def _():
            arrived(column(z - step), part)
            pass_on(z - step, part, True, False)

        @pl.when(z + step < FAR)
        def _():
            arrived(column(z + step), part)
            pass_on(z + step, part, False, True)

    def gather_end(part):
        for row in range(FAR):
            for col in range(SIDE):
                arrived(row * 4 + col * 2 + 1 - c, part)
        own_copy(part).wait()

    def gather_sent(part):
        for row in range(FAR):
            copy(column(row), part, gather_side.at[row, part], across).wait_send()
            for which in range(2):
                copy(column(row), part, gather_core.at[which, row, part], sibling).wait_send()

            @pl.when((z < FAR - 1) & (z >= row))
            def _(row=row):
                copy(column(row), part, gather_up.at[row, part], up).wait_send()

            @pl.when((z > 0) & (z <= row))
            def _(row=row):
                copy(column(row), part, gather_down.at[row, part], down).wait_send()

    def named(slot):
        entry = 0
        for i in range(1, listed):
            entry = jnp.where(chosen[i] == slot, i, entry)
        return entry

    def attend(part, *between):
        fetched = blocks[part]
        keys = jnp.concatenate([fetched[block, 0] for block in chosen], axis=0)
        values = jnp.concatenate([fetched[block, 1] for block in chosen], axis=0)
        keys_t, values_t = keys.T, values.T
        for pair in range(pairs):
            first = part * grouped + 2 * pair
            spans = [pl.ds(first + i, rows, stride=heads) for i in range(2)]
            query = jnp.concatenate([qf[s, :] for s in spans], axis=0).astype(HALF)
            grad = jnp.concatenate([gf[s, :] for s in spans], axis=0).astype(HALF)
            scores = nt(keys, query)
            top = jnp.max(scores, axis=0, keepdims=True)
            weights = jnp.exp((scores - top) * scale)
            weights = weights * (1.0 / jnp.sum(weights, axis=0, keepdims=True))
            probs = weights.astype(HALF)
            out = nn(values_t, probs).T
            grad_probs = nt(values, grad)
            deltas = jnp.sum(weights * grad_probs, axis=0, keepdims=True)
            grad_scores = (weights * (grad_probs - deltas)).astype(HALF)
            grad_query = (nn(keys_t, grad_scores) * scale).T
            for i, s in enumerate(spans):
                af[s, :] = out[i * rows : (i + 1) * rows]
                df[s, :] = grad_query[i * rows : (i + 1) * rows]
            key_terms = nn(grad_scores, query).reshape(listed, rows, width)
            value_terms = nn(probs, grad).reshape(listed, rows, width)
            if pair == 0:
                sums[:, 0] = key_terms
                sums[:, 1] = value_terms
            else:
                sums[:, 0] += key_terms
                sums[:, 1] += value_terms
            for action, *at in between[pair] if pair < len(between) else ():
                action(*at)
        for which, factor in ((0, scale), (1, 1.0)):
            own[part, which] = sums[0, which] * factor
            for i in range(1, listed):
                total = sums[i, which]
                for j in range(1, listed):
                    if j != i:
                        same = chosen[j] == chosen[i]
                        total = total + jnp.where(same, sums[j, which], 0.0)
                merged[i, which] = total * factor
            merged[0, which] = jnp.zeros((rows, width), FLOAT)
        for row in range(FAR):
            for col in range(SIDE):
                slot = row * 4 + col * 2
                keep[part, row, col] = merged[named(slot + c)]
                give[part, row, col] = merged[named(slot + 1 - c)].astype(HALF)

    def core_copy(row, col, part):
        return remote(
            give.at[part, row, col], from_core.at[part, row, col],
            core_send.at[part, row, col], core_recv.at[part, row, col], sibling,
        )

    def side_copy(row, part):
        return remote(
            to_side.at[part, row], from_side.at[part, row],
            side_send.at[part, row], side_recv.at[part, row], across,
        )

    def up_copy(row, part):
        return remote(
            to_row.at[part, row], from_down.at[part, row],
            row_send.at[part, row], down_recv.at[part, row], up,
        )

    def down_copy(row, part):
        return remote(
            to_row.at[part, row], from_up.at[part, row],
            row_send.at[part, row], up_recv.at[part, row], down,
        )

    order = [pick(codes, z) for codes in ORDER]

    def core_start(part):
        for row in order:
            core_copy(row, 1 - x, part).start()
        for row in order:
            core_copy(row, x, part).start()

    def side_step(step, part):
        row = order[step]
        core_copy(row, 1 - x, part).wait_recv()
        to_side[part, row] = (
            keep[part, row, 1 - x] + from_core[part, row, 1 - x].astype(FLOAT)
        ).astype(HALF)
        side_copy(row, part).start()

    def row_step(step, part):
        row = order[step]
        core_copy(row, x, part).wait_recv()
        side_copy(row, part).wait_recv()
        acc[...] = (
            keep[part, row, x]
            + from_core[part, row, x].astype(FLOAT)
            + from_side[part, row].astype(FLOAT)
        )

        @pl.when((row >= z) & (z > 0))
        def _():
            up_copy(row, part).wait_recv()
            acc[...] += from_down[part, row].astype(FLOAT)

        @pl.when((row <= z) & (z < FAR - 1))
        def _():
            down_copy(row, part).wait_recv()
            acc[...] += from_up[part, row].astype(FLOAT)

        if step < FAR - 1:
            to_row[part, row] = acc[...].astype(HALF)

            @pl.when(row > z)
            def _():
                up_copy(row, part).start()

            @pl.when(row < z)
            def _():
                down_copy(row, part).start()
        else:
            dk_ref[part] = (acc[0] + own[part, 0]).astype(HALF)
            dv_ref[part] = (acc[1] + own[part, 1]).astype(HALF)

    def sum_sent(part):
        for step, row in enumerate(order):
            side_copy(row, part).wait_send()
            for col in range(SIDE):
                core_copy(row, col, part).wait_send()
            if step < FAR - 1:
                up_copy(row, part).wait_send()

    def side_steps(part):
        for step in range(FAR):
            side_step(step, part)

    start, hop, shares = gather_start, gather_step, gather_shares
    greet(me, z, x, c)
    start(0)
    start(1)
    gf[...] = g_ref[...].astype(FLOAT)
    hop(1, 0)
    shares(0, 0)
    hop(2, 0)
    shares(1, 0)
    hop(3, 0)
    start(2)
    qf[...] = q_ref[...].astype(FLOAT)
    shares(2, 0)
    hop(1, 1)
    shares(0, 1)
    hop(2, 1)
    shares(3, 0)
    gather_end(0)
    attend(
        0,
        [(hop, 3, 1), (start, 3), (shares, 1, 1)],
        [(hop, 1, 2), (shares, 0, 2), (shares, 2, 1), (hop, 2, 2)],
        [(shares, 3, 1), (hop, 3, 2), (hop, 1, 3), (shares, 1, 2)],
    )
    core_start(0)
    gather_end(1)
    attend(
        1,
        [(hop, 2, 3), (shares, 2, 2), (shares, 0, 3), (side_steps, 0)],
        [(shares, 3, 2), (hop, 3, 3), (shares, 1, 3)],
        [(shares, 2, 3), (row_step, 0, 0)],
    )
    core_start(1)
    gather_end(2)
    attend(
        2,
        [(shares, 3, 3), (side_steps, 1)],
        [(row_step, 1, 0), (row_step, 2, 0)],
        [(row_step, 3, 0), (row_step, 0, 1)],
    )
    core_start(2)
    gather_end(3)
    attend(
        3,
        [(side_steps, 2), (row_step, 1, 1)],
        [(row_step, 2, 1), (row_step, 3, 1)],
        [(row_step, 0, 2), (row_step, 1, 2)],
    )
    core_start(3)
    row_step(2, 2)
    side_steps(3)
    row_step(3, 2)
    att_ref[...] = af[...].astype(HALF)
    dq_ref[...] = df[...].astype(HALF)
    for step in range(FAR):
        row_step(step, 3)
    for part in range(parts):
        gather_sent(part)
        sum_sent(part)


def layer(offsets, masks, global_blocks, query_rows, grad_rows, kv):
    total, width = query_rows.shape
    parts, _, rows, _ = kv.shape
    listed = 1 + offsets.shape[0] + masks.shape[0] + global_blocks.shape[0]
    tile = kv.shape[1:]
    dma = pltpu.SemaphoreType.DMA
    whole = pl.BlockSpec(memory_space=pltpu.VMEM)
    scalars = pl.BlockSpec(memory_space=pltpu.SMEM)
    slots = pltpu.VMEM((parts, FAR, *tile), HALF)
    long = pltpu.VMEM((total, width), FLOAT)
    fetched = pltpu.VMEM((FAR * SIDE * CORES, *tile), HALF)
    by_slot = (parts, FAR, SIDE)
    grad_shape = jax.ShapeDtypeStruct((parts, rows, width), HALF)
    return pl.pallas_call(
        layer_kernel,
        out_shape=(
            jax.ShapeDtypeStruct((total, width), HALF),
            jax.ShapeDtypeStruct((total, width), HALF),
            grad_shape,
            grad_shape,
        ),
        in_specs=[scalars, scalars, scalars, whole, whole, whole],
        out_specs=(whole,) * 4,
        scratch_shapes=[
            long, long, long, long,
            pltpu.VMEM((listed, 2, rows, width), FLOAT),
            pltpu.VMEM((listed, 2, rows, width), FLOAT),
            fetched, fetched, fetched, fetched,
            pltpu.VMEM(kv.shape, FLOAT),
            pltpu.VMEM((*by_slot, *tile), FLOAT),
            pltpu.VMEM((*by_slot, *tile), HALF),
            pltpu.VMEM((*by_slot, *tile), HALF),
            slots, slots, slots, slots, slots,
            pltpu.VMEM(tile, FLOAT),
            dma((parts,)), dma((FAR, parts)), dma((2, FAR, parts)), dma((FAR, parts)),
            dma((FAR, parts)), dma((FAR * SIDE * CORES, parts)),
            dma(by_slot), dma((parts, FAR)), dma((parts, FAR)),
            dma(by_slot), dma((parts, FAR)), dma((parts, FAR)), dma((parts, FAR)),
        ],
        compiler_params=pltpu.CompilerParams(
            collective_id=0, has_side_effects=True, vmem_limit_bytes=56 * 2**20
        ),
    )(offsets, masks, global_blocks, query_rows, grad_rows, kv)


def local(queries, key_heads, value_heads, grad_out, offsets, random_masks, global_blocks):
    rows, heads, width = queries.shape
    kv = jnp.stack([key_heads, value_heads]).transpose(2, 0, 1, 3)
    attended, grad_queries, grad_keys, grad_values = layer(
        offsets, random_masks, global_blocks,
        queries.reshape(rows * heads, width), grad_out.reshape(rows * heads, width), kv,
    )
    return (
        attended.reshape(queries.shape),
        grad_queries.reshape(queries.shape),
        grad_keys.transpose(1, 0, 2),
        grad_values.transpose(1, 0, 2),
    )


def solution(mesh):
    return jax.shard_map(
        local if mesh.shape["seq"] == FAR * SIDE * CORES else local_any,
        mesh=mesh,
        in_specs=(
            P(("groups", "seq"), None, None),
            P(("groups", "seq"), None, None),
            P(("groups", "seq"), None, None),
            P(("groups", "seq"), None, None),
            P(),
            P(),
            P(),
        ),
        out_specs=(
            P(("groups", "seq"), None, None),
            P(("groups", "seq"), None, None),
            P(("groups", "seq"), None, None),
            P(("groups", "seq"), None, None),
        ),
        check_vma=False,
    )
```
